512 devices in a mesh: band: 128 (over y, z, core), edge: 4 (over x).
Axes of the slice: x: 4, y: 4, z: 16, core: 2. Of those that a mesh axis runs over, the one named last changes fastest.
Arguments:
- grid_lat: bfloat16 [131072, 512], P('band'), may hold values from -6 to 6
- edge_lat: bfloat16 [65536, 512], P(('band', 'edge')), may hold values from -24 to 24
- send_local: int32 [65536], P(('band', 'edge')), may hold values from 0 to 1023
- dest_band: int32 [65536, 1], P(('band', 'edge')), may hold values from 0 to 127; in each aligned block of 128 rows (0 to 127, 128 to 255, ...) at most 2 rows name the same one
- receiver_in_band: int32 [65536], P(('band', 'edge')), may hold values from 0 to 255
- mesh_lat: bfloat16 [32768, 512], P('band'), may hold values from -6 to 6
- w_edge_in: bfloat16 [512, 512], replicated, may hold values from -0.25 to 0.25
- w_edge_out: bfloat16 [512, 512], replicated, may hold values from -0.25 to 0.25
- w_node_in: bfloat16 [1024, 512], P(None, 'edge'), may hold values from -0.1875 to 0.1875
- w_node_out: bfloat16 [512, 512], P('edge'), may hold values from -0.25 to 0.25
- norm_gain: float32 [512], replicated, may hold values from 0.25 to 1.75
- cotangent: bfloat16 [32768, 512], P('band'), may hold values from -6 to 6
Outputs:
- new_mesh: bfloat16 [32768, 512], P('band')
- grad_edge_in: float32 [512, 512], P(('band', 'edge'))
- grad_edge_out: float32 [512, 512], P(('band', 'edge'))
The draws below stay inside these ranges and needn't reach their ends.
Inputs may be any that keep to these rules, and one draw needn't show every extreme that they name: Among the 128 edges of one device at most 2 have any one band in dest_band; in some devices one band has exactly 2.
All inputs are finite; a program needn't handle non-finite values.
Results may differ from the reference program's by a relative error of at most 0.02.
Values may be sent and summed in bfloat16 or wider, within the bound.
A program may use at most 64 MiB of HBM per device.

```python
import math
import jax
import jax.numpy as jnp
import numpy as np
from jax import lax

D = 512
H = 512
G_BAND = 1024
M_BAND = 256
E_DEV = 128
CAP = 2
NG = 131072
NM = 32768
NE = 65536
N_BAND = 128
N_EDGE = 4


def place_ends(array, own_key, least, high):
    place = [jax.random.randint(jax.random.fold_in(own_key, axis), (), 0, length) for axis, length in enumerate(array.shape)]
    widest = array.shape.index(max(array.shape))
    next_to = place[:widest] + [(place[widest] + 1) % array.shape[widest]] + place[widest + 1:]
    return array.at[tuple(place)].set(least).at[tuple(next_to)].set(high)


def strengthened(drawn, own_key, source, target, blocks, factor):
    def block_of(dim):
        return (jnp.arange(drawn.shape[dim]) // (drawn.shape[dim] // blocks)).reshape((-1,) + (1,) * (drawn.ndim - 1 - dim))

    one_side = jax.random.permutation(own_key, blocks)[block_of(target)]
    second = (block_of(target) + blocks // 2) % blocks
    return jnp.where((block_of(source) == one_side) | (block_of(source) == second), factor * drawn, drawn)


def steps_of(rng, extent, pieces, smallest, largest):
    def one(axis_at, blocks):
        steps = jax.random.uniform(jax.random.fold_in(jax.random.fold_in(rng, 6), axis_at), (blocks,), jnp.float32, smallest / len(pieces), largest / len(pieces))
        return jnp.repeat(jnp.exp(steps), extent[axis_at] // blocks).reshape((-1,) + (1,) * (len(extent) - axis_at - 1))

    level = one(*pieces[0])
    for cut in pieces[1:]:
        level = level * one(*cut)
    return level


def assign_block(rng, own, number, rows, number_of, top, limit, lean):
    order = jax.random.permutation(rng, number_of)
    packed, common = portions_of(number_of, rows * top, limit, lean, True), portions_of(number_of, rows * top, limit, lean, False)
    places = jnp.arange(number_of)

    def named(lengths, turn):
        used = int((lengths > 0).sum())
        fixed = max(1, used // 4)
        shifted = fixed + (places - fixed + turn * (used - fixed)) % max(1, number_of - fixed)
        return jnp.zeros((number_of,), jnp.int32).at[order[jnp.where(places < fixed, places, shifted)]].set(jnp.asarray(lengths, jnp.int32))

    lengths = jnp.where(number % 4 == 0, named(packed, number // 4), named(common, number - number // 4 - 1))
    mixed = jax.random.permutation(jax.random.fold_in(own, 3), number_of)
    source_of, sink = mixed[0:number_of // 2 * 2:2], mixed[1:number_of // 2 * 2:2]
    room = jnp.minimum(lengths[source_of] - 1, limit - lengths[sink]) // 2
    room = jnp.where((source_of == order[0]) | (sink == order[0]) | (lengths[sink] == 0), 0, jnp.maximum(room, 0))
    shifted = jax.random.randint(jax.random.fold_in(own, 4), (number_of // 2,), 0, 1 << 20) % (room + 1)
    lengths = lengths.at[source_of].add(-shifted).at[sink].add(shifted)
    labels = jnp.searchsorted(jnp.cumsum(lengths), jnp.arange(rows * top), side="right").astype(jnp.int32)
    table = labels.reshape(top, rows).T
    table = table[jax.random.permutation(jax.random.fold_in(own, 1), rows)]
    turn = jax.random.randint(jax.random.fold_in(own, 2), (rows, 1), 0, top)
    return jnp.take_along_axis(table, (jnp.arange(top)[None, :] + turn) % top, axis=1)


def portions_of(count, total, limit, slope, full):
    portions = [(1 << 20) // math.isqrt(standing ** slope) + 1 for standing in range(1, count + 1)]
    largest = limit if full else min(limit, max(-(-total // count), total * portions[0] // sum(portions)))
    least = 1 if total - largest >= count - 1 else 0
    given, surplus = [largest] + [least] * (count - 1), total - largest - least * (count - 1)
    while surplus > 0:
        candidates = [i for i in range(1, count) if given[i] < largest] or [i for i in range(1, count) if given[i] < limit]
        mass, left = sum([portions[i] for i in candidates]), surplus
        for i in candidates:
            more = min(limit - given[i], max(1, left * portions[i] // mass), surplus)
            given[i] = given[i] + more
            surplus = surplus - more
    return np.array(given)


def noise(stream_key, extent, spread, most, split=(), kind=jnp.bfloat16):
    values = spread * jax.random.normal(stream_key, extent, jnp.float32)
    if split:
        values = values * steps_of(stream_key, extent, split, -0.22, 0.18)
    return jnp.clip(values, -most, most).astype(kind)


def noise_with(own_key, dims, deviation, limit, pieces, heavy, held_as=jnp.bfloat16):
    result = deviation * jax.random.normal(own_key, dims, jnp.float32)
    if pieces:
        result = result * steps_of(own_key, dims, pieces, -0.22, 0.18)
    return jnp.clip(strengthened(result, jax.random.fold_in(own_key, 3), *heavy), -limit, limit).astype(held_as)


def setup_inputs(seed: int = 0) -> dict:
    key_list = jax.random.split(jax.random.key(seed), 13)
    grid_lat = noise(key_list[0], (NG, D), 1.0, 6.0, ((0, 128),))
    edge_lat = noise_with(key_list[1], (NE, D), 1.0, 24.0, ((0, 512),), (0, 1, 512, 6.0))
    send_local = place_ends(jax.random.randint(key_list[2], (NE,), 0, G_BAND), jax.random.fold_in(key_list[2], 1), 0, G_BAND - 1).astype(jnp.int32)
    dest_band_keys = jax.random.split(jax.random.fold_in(key_list[3], 1), NE // E_DEV)
    dest_band_turns = jax.random.permutation(jax.random.fold_in(key_list[3], 3), NE // E_DEV)
    dest_band = jax.vmap(lambda own, number: assign_block(jax.random.fold_in(key_list[3], 2), own, number, E_DEV, N_BAND, 1, CAP, 2))(dest_band_keys, dest_band_turns).reshape((NE, 1))
    receiver_in_band = place_ends(jax.random.randint(key_list[4], (NE,), 0, M_BAND), jax.random.fold_in(key_list[4], 1), 0, M_BAND - 1).astype(jnp.int32)
    mesh_lat = noise(key_list[5], (NM, D), 1.0, 6.0, ((0, 128),))
    w_edge_in = noise(key_list[6], (D, H), D ** -0.5, 0.25)
    w_edge_out = noise(key_list[7], (D, H), H ** -0.5, 0.25)
    w_node_in = noise(key_list[8], (2 * D, H), (2 * D) ** -0.5, 0.1875, ((1, 4),))
    w_node_out = noise(key_list[9], (H, D), H ** -0.5, 0.25, ((0, 4),))
    norm_gain = jnp.clip(1.0 + 0.15 * jax.random.normal(key_list[10], (D,), jnp.float32), 0.25, 1.75)
    cotangent = noise(key_list[11], (NM, D), 1.0, 6.0, ((0, 128),))
    return {"grid_lat": grid_lat, "edge_lat": edge_lat, "send_local": send_local, "dest_band": dest_band, "receiver_in_band": receiver_in_band, "mesh_lat": mesh_lat, "w_edge_in": w_edge_in, "w_edge_out": w_edge_out, "w_node_in": w_node_in, "w_node_out": w_node_out, "norm_gain": norm_gain, "cotangent": cotangent}


def swish_grad(value):
    sig = jax.nn.sigmoid(value)
    return sig * (1.0 + value * (1.0 - sig))

def reference(grid_lat, edge_lat, send_local, dest_band, receiver_in_band, mesh_lat, w_edge_in, w_edge_out, w_node_in, w_node_out, norm_gain, cotangent):
    edge_list = edge_lat.shape[0]
    band_of = jnp.arange(edge_list, dtype=jnp.int32) // (E_DEV * N_EDGE)
    senders = (band_of * G_BAND + send_local).astype(jnp.int32)
    receivers = (dest_band[:, 0] * M_BAND + receiver_in_band).astype(jnp.int32)
    x_in = (grid_lat[senders].astype(jnp.float32) + edge_lat.astype(jnp.float32)).astype(jnp.bfloat16)
    z_edge = jnp.dot(x_in, w_edge_in, preferred_element_type=jnp.float32)
    h_edge = jax.nn.silu(z_edge).astype(jnp.bfloat16)
    message = jnp.dot(h_edge, w_edge_out.T, preferred_element_type=jnp.float32).astype(jnp.bfloat16)
    agg = jax.ops.segment_sum(message.astype(jnp.float32), receivers, num_segments=NM).astype(jnp.bfloat16)
    joined = jnp.concatenate([mesh_lat, agg], axis=1)
    z_node = jnp.dot(joined, w_node_in, preferred_element_type=jnp.float32)
    h_node = jax.nn.silu(z_node).astype(jnp.bfloat16)
    y_out = jnp.dot(h_node, w_node_out, preferred_element_type=jnp.float32)
    mean_y = lax.optimization_barrier(jnp.mean(y_out, axis=1, keepdims=True))
    centred = y_out - mean_y
    inv_std = lax.rsqrt(lax.optimization_barrier(jnp.mean(centred * centred, axis=1, keepdims=True)) + 1e-05)
    normed = centred * inv_std
    new_mesh = (mesh_lat.astype(jnp.float32) + normed * norm_gain).astype(jnp.bfloat16)
    upstream = cotangent.astype(jnp.float32) * norm_gain
    d_y = (upstream - lax.optimization_barrier(jnp.mean(upstream, axis=1, keepdims=True)) - normed * lax.optimization_barrier(jnp.mean(upstream * normed, axis=1, keepdims=True))) * inv_std
    d_y = d_y.astype(jnp.bfloat16)
    dh_node = jnp.dot(d_y, w_node_out.T, preferred_element_type=jnp.float32)
    dz_node = (dh_node * swish_grad(z_node)).astype(jnp.bfloat16)
    d_agg = jnp.dot(dz_node, w_node_in[D:, :].T, preferred_element_type=jnp.float32).astype(jnp.bfloat16)
    message_gradient = d_agg[receivers]
    dh_edge = jnp.dot(message_gradient, w_edge_out, preferred_element_type=jnp.float32)
    dz_edge = (dh_edge * swish_grad(z_edge)).astype(jnp.bfloat16)
    grad_edge_in = jnp.dot(x_in.T, dz_edge, preferred_element_type=jnp.float32)
    grad_edge_out = jnp.dot(message_gradient.T, h_edge, preferred_element_type=jnp.float32)
    return (new_mesh, grad_edge_in, grad_edge_out)
```

```python
import jax
import jax.numpy as jnp
from jax import lax
from jax.experimental import pallas as pl
from jax.experimental.pallas import tpu as pltpu
from jax.sharding import PartitionSpec as P

BF = jnp.bfloat16
F32 = jnp.float32
I32 = jnp.int32
MESH = pl.DeviceIdType.MESH

Z_AT = (0, 1, 15, 2, 14, 3, 13, 4, 12, 5, 11, 6, 10, 7, 9, 8)
Z_SEND = (8, 7, 9, 6, 10, 5, 11, 4, 12, 3, 13, 2, 14, 1, 15)
GROUPS = 4


def iota(shape, axis):
    return lax.broadcasted_iota(I32, shape, axis)


def one_hot(cond):
    return jnp.where(cond, 1.0, 0.0).astype(BF)


def mm(a, b):
    return jnp.dot(a, b, preferred_element_type=F32)


def mm_nt(a, b):
    return lax.dot_general(a, b, (((1,), (1,)), ((), ())), preferred_element_type=F32)


def mm_tn(a, b):
    return lax.dot_general(a, b, (((0,), (0,)), ((), ())), preferred_element_type=F32)


def row_order(shape, axis, x_first):
    p = iota(shape, axis)
    core, high, low, z = p >> 8, (p >> 6) & 3, (p >> 4) & 3, p & 15
    x, y = (high, low) if x_first else (low, high)
    return y * 128 + z * 8 + core * 4 + x


def kernel(
    grid_ref, edge_ref, send_ref, dest_ref, recv_ref, mesh_ref, wei_ref, weo_ref, wni_ref, wno_ref, gain_ref, cot_ref,
    new_ref, gin_ref, gout_ref,
    s1_src, s1_dst, c1_src, c1_dst, z_src, zc_src, zc_dst, xall, rx,
    wni, wno, sgrad, hid, nm,
    co_src, co_dst, ci_src, ci_dst, oy_src, oy_dst, ix_src, ix_dst, ox_src, ox_dst, iy_src, iy_dst,
    oz_src, oz_dst, iz_src, iz_dst, acc_o, acc_i, mid_o, mid_i,
    s_yc, s_yc_c, s_z, s_z_c, s_xf, s_rx, s_w, s_nm, s_core, s_r1, s_r2, s_rz,
):
    band = lax.axis_index("band")
    x = lax.axis_index("edge")
    y, z, c = band >> 5, (band >> 1) & 15, band & 1

    def at(ty, tz, tc, tx):
        return (((ty & 3) * 16 + (tz & 15)) * 2 + (tc & 1), tx & 3)

    def copy(src, dst, sems, i, target):
        return pltpu.make_async_remote_copy(
            src_ref=src, dst_ref=dst, send_sem=sems.at[0, i], recv_sem=sems.at[1, i],
            device_id=target, device_id_type=MESH,
        )

    barrier = pltpu.get_barrier_semaphore()
    greeted = [at(y, z + i, c, x) for i in Z_SEND]
    greeted += [at(y + i // 2, z, c + i % 2, x) for i in range(1, 8)]
    greeted += [at(y, z, c, x + i) for i in range(1, 4)]
    for other in greeted:
        pl.semaphore_signal(barrier, inc=1, device_id=other, device_id_type=MESH)

    eye = iota((128, 128), 0) == iota((128, 128), 1)
    dest = dest_ref[...]
    dest_b = jnp.broadcast_to(dest, (128, 128)).astype(F32)
    dest_col = jnp.sum(jnp.where(eye, dest_b, 0.0), axis=1, keepdims=True)
    earlier = (dest_col == dest_b) & (iota((128, 128), 0) < iota((128, 128), 1))
    rank = jnp.sum(jnp.where(earlier, 1.0, 0.0), axis=0, keepdims=True).astype(I32)
    slot = ((dest >> 5) * 2 + (dest & 1)) * 32 + ((dest >> 1) & 15) * 2 + rank
    code = ((dest * 2 + rank) * 256 + recv_ref[...]).astype(F32)
    send_b = jnp.broadcast_to(send_ref[...], (128, 128)).astype(F32)
    send_col = jnp.sum(jnp.where(eye, send_b, 0.0), axis=1, keepdims=True).astype(I32)
    pick = one_hot(send_col == iota((128, 1024), 1))
    x_in = (mm(pick, grid_ref[...]) + edge_ref[...].astype(F32)).astype(BF)
    order_in = one_hot(iota((512, 512), 1) == row_order((512, 512), 0, True))
    x_in = mm_nt(x_in, order_in).astype(BF)
    place = one_hot(iota((256, 128), 0) == slot)
    slots = mm(place, x_in).astype(BF)
    for i in range(8):
        s1_src[i] = slots[32 * i : 32 * (i + 1)]
    c1_src[...] = code

    pl.semaphore_wait(barrier, len(greeted))

    s1 = []
    for i in (4, 5, 2, 3, 6, 7, 1):
        ty, tc = y + i // 2, c + i % 2
        target = at(ty, z, tc, x)
        s1.append(copy(c1_src, c1_dst.at[i], s_yc_c, i, target))
        s1.append(copy(s1_src.at[(ty & 3) * 2 + (tc & 1)], s1_dst.at[i], s_yc, i, target))
    for d in s1:
        d.start()
    lanes = pl.ds(pl.multiple_of(x * 128, 128), 128)
    weights = []
    for i in (2, 1, 3):
        target = at(y, z, c, x + i)
        weights.append(copy(wni_ref, wni.at[:, lanes], s_w, i, target))
        weights.append(copy(wno_ref, wno.at[lanes, :], s_w, 4 + i, target))
    for d in weights:
        d.start()
    s1_dst[0] = s1_src[y * 2 + c]
    c1_dst[0] = c1_src[...]
    wni[:, lanes] = wni_ref[...]
    wno[lanes, :] = wno_ref[...]

    w_in = mm(order_in, wei_ref[...]).astype(BF)
    order_out = one_hot(iota((512, 512), 1) == row_order((512, 512), 0, False))
    w_out = mm(order_out, weo_ref[...]).astype(BF)
    o = iota((256, 256), 0)
    regroup = one_hot(iota((256, 256), 1) == (o & 7) * 32 + (o >> 4) * 2 + ((o >> 3) & 1))
    l = iota((256, 256), 1)
    to_rows = one_hot(iota((256, 256), 0) == ((l >> 3) & 1) * 128 + (l >> 4) * 8 + (l & 7))

    for d in s1:
        d.wait_recv()
    gathered = mm(regroup, s1_dst[...].reshape(256, 512)).astype(BF)
    for i in range(16):
        z_src[i] = gathered[16 * i : 16 * (i + 1)]
    zc_src[...] = jnp.concatenate([c1_dst[i] for i in range(8)], axis=0)
    s2 = {}
    for i in Z_SEND:
        p = Z_AT.index(i)
        target = at(y, z + i, c, x)
        s2[p] = (
            copy(zc_src, zc_dst.at[p], s_z_c, p, target),
            copy(z_src.at[(z + i) & 15], xall.at[0, p], s_z, p, target),
        )
        for d in s2[p]:
            d.start()
    xall[0, 0] = z_src[z]
    zc_dst[0] = zc_src[...]

    def edge_rows(plane, group):
        rows = xall[plane, pl.ds(4 * group, 4)].reshape(64, 512)
        z_edge = mm(rows, w_in)
        sig = jax.nn.sigmoid(z_edge)
        at_rows = pl.ds(plane * 256 + group * 64, 64)
        hid[at_rows, :] = (z_edge * sig).astype(BF)
        sgrad[at_rows, :] = sig * (1.0 + z_edge * (1.0 - sig))

    forward = []
    for g in range(GROUPS):
        for p in range(4 * g, 4 * g + 4):
            if p:
                for d in s2[p]:
                    d.wait_recv()
        part = pl.ds(4 * g, 4)
        sent = [copy(xall.at[0, part], xall.at[i, part], s_xf, g * 4 + i, at(y, z, c, x + i)) for i in (2, 1, 3)]
        for d in sent:
            d.start()
        forward.append(sent)
        edge_rows(0, g)

    codes = zc_dst[...].reshape(128, 128)
    found = []
    for r in range(2):
        off = codes - ((band * 2 + r) * 256).astype(F32)
        mine = jnp.where((off >= 0.0) & (off < 256.0), off + 1.0, 0.0).astype(BF)
        found.append(mm_nt(jnp.ones((8, 128), BF), mine))
    rx[0] = mm(jnp.concatenate(found, axis=1).astype(BF), to_rows)
    sent_rx = [copy(rx.at[0], rx.at[i], s_rx, i, at(y, z, c, x + i)) for i in (2, 1, 3)]
    for d in sent_rx:
        d.start()

    for d in weights:
        d.wait_recv()
    nodes = pl.ds(pl.multiple_of(x * 64, 64), 64)
    mesh = mesh_ref[nodes, :]
    z_mesh = mm(mesh, wni[0:512, :])
    w_bot = mm(order_out, wni[512:1024, :]).astype(BF)

    for g in range(GROUPS):
        for d in forward[g]:
            d.wait_recv()
        for plane in range(1, 4):
            edge_rows(plane, g)
    for d in sent_rx:
        d.wait_recv()

    node = iota((64, 256), 0).astype(F32) + (x * 64 + 1).astype(F32)
    collect = jnp.concatenate([one_hot(rx[i][0:1, :] == node) for i in range(4)], axis=1)
    agg_h = mm(collect, hid[...]).astype(BF)
    agg = mm_nt(agg_h, w_out).astype(BF)
    z_node = z_mesh + mm(agg, w_bot)
    sig = jax.nn.sigmoid(z_node)
    h_node = (z_node * sig).astype(BF)
    y_out = mm(h_node, wno[...])
    gain = gain_ref[...]
    mean_y = jnp.mean(y_out, axis=1, keepdims=True)
    centred = y_out - mean_y
    inv_std = lax.rsqrt(jnp.mean(centred * centred, axis=1, keepdims=True) + 1e-05)
    normed = centred * inv_std
    nm[nodes, :] = (mesh.astype(F32) + normed * gain).astype(BF)
    sent_nm = [copy(nm.at[nodes, :], nm.at[nodes, :], s_nm, i, at(y, z, c, x + i)) for i in (2, 1, 3)]
    for d in sent_nm:
        d.start()
    up = cot_ref[nodes, :].astype(F32) * gain
    d_y = (
        up - jnp.mean(up, axis=1, keepdims=True) - normed * jnp.mean(up * normed, axis=1, keepdims=True)
    ) * inv_std
    dh_node = mm_nt(d_y.astype(BF), wno[...])
    dz_node = (dh_node * (sig * (1.0 + z_node * (1.0 - sig)))).astype(BF)
    d_agg = mm_nt(dz_node, w_bot).astype(BF)
    dh = mm(d_agg, w_out).astype(BF)

    keep = pl.ds(pl.multiple_of(c * 256, 256), 256)
    give = pl.ds(pl.multiple_of((1 - c) * 256, 256), 256)
    other = at(y, z, c + 1, x)
    acc_o[...] = mm_tn(d_agg, agg_h)
    co_src[...] = acc_o[give, :].astype(BF)
    core_o = copy(co_src, co_dst, s_core, 0, other)
    core_o.start()
    d_edge = (mm_tn(collect, dh) * sgrad[...]).astype(BF)
    ci_src[...] = mm_tn(xall[:, :, :, give].reshape(1024, 256), d_edge).astype(BF)
    core_i = copy(ci_src, ci_dst, s_core, 1, other)
    core_i.start()

    core_o.wait_recv()
    acc_o[keep, :] += co_dst[...].astype(F32)
    oy_src[...] = acc_o[keep, :].astype(BF).reshape(4, 64, 512)
    sent_oy = [copy(oy_src.at[(y + i) & 3], oy_dst.at[i], s_r1, i, at(y + i, z, c, x)) for i in (2, 1, 3)]
    for d in sent_oy:
        d.start()
    acc_i[...] = mm_tn(xall[:, :, :, keep].reshape(1024, 256), d_edge)
    core_i.wait_recv()
    acc_i[...] += ci_dst[...].astype(F32)
    ix_src[...] = acc_i[...].astype(BF).reshape(4, 64, 512)
    sent_ix = [copy(ix_src.at[(x + i) & 3], ix_dst.at[i], s_r1, 4 + i, at(y, z, c, x + i)) for i in (2, 1, 3)]
    for d in sent_ix:
        d.start()

    for d in sent_oy:
        d.wait_recv()
    total = acc_o[pl.ds(pl.multiple_of(c * 256 + y * 64, 64), 64), :]
    for i in range(1, 4):
        total += oy_dst[i].astype(F32)
    mid_o[...] = total
    ox_src[...] = total.astype(BF).reshape(4, 16, 512)
    sent_ox = [copy(ox_src.at[(x + i) & 3], ox_dst.at[i], s_r2, i, at(y, z, c, x + i)) for i in (2, 1, 3)]
    for d in sent_ox:
        d.start()
    for d in sent_ix:
        d.wait_recv()
    total = acc_i[pl.ds(pl.multiple_of(x * 64, 64), 64), :]
    for i in range(1, 4):
        total += ix_dst[i].astype(F32)
    mid_i[...] = total
    iy_src[...] = total.astype(BF).reshape(4, 16, 512)
    sent_iy = [copy(iy_src.at[(y + i) & 3], iy_dst.at[i], s_r2, 4 + i, at(y + i, z, c, x)) for i in (2, 1, 3)]
    for d in sent_iy:
        d.start()

    def last(mid, here, sent, dst, src_z, dst_z, base):
        for d in sent:
            d.wait_recv()
        rows = mid[pl.ds(pl.multiple_of(here * 16, 16), 16), :]
        for i in range(1, 4):
            rows += dst[i].astype(F32)
        for i in range(16):
            src_z[i] = rows[i : i + 1]
        out = []
        for i in Z_SEND:
            out.append(copy(src_z.at[(z + i) & 15], dst_z.at[i], s_rz, base + i, at(y, z + i, c, x)))
            out[-1].start()
        return out

    sent_oz = last(mid_o, x, sent_ox, ox_dst, oz_src, oz_dst, 0)
    sent_iz = last(mid_i, y, sent_iy, iy_dst, iz_src, iz_dst, 16)

    for d in sent_nm:
        d.wait_recv()
    new_ref[...] = nm[...]

    def finish(sent, src_z, dst_z, out_ref):
        for d in sent:
            d.wait_recv()
        total = src_z[z]
        for i in range(1, 16):
            total += dst_z[i]
        out_ref[...] = total

    finish(sent_oz, oz_src, oz_dst, gout_ref)
    finish(sent_iz, iz_src, iz_dst, gin_ref)

    everything = s1 + weights + [d for pair in s2.values() for d in pair] + [d for sent in forward for d in sent]
    everything += sent_rx + sent_nm + [core_o, core_i] + sent_oy + sent_ix + sent_ox + sent_iy + sent_oz + sent_iz
    for d in everything:
        d.wait_send()


def body(
    grid_lat, edge_lat, send_local, dest_band, receiver_in_band, mesh_lat,
    w_edge_in, w_edge_out, w_node_in, w_node_out, norm_gain, cotangent,
):
    vmem = pl.BlockSpec(memory_space=pltpu.VMEM)
    dma = pltpu.SemaphoreType.DMA
    new_mesh, grad_in, grad_out = pl.pallas_call(
        kernel,
        out_shape=(
            jax.ShapeDtypeStruct((256, 512), BF),
            jax.ShapeDtypeStruct((1, 512), F32),
            jax.ShapeDtypeStruct((1, 512), F32),
        ),
        in_specs=[vmem] * 12,
        out_specs=(vmem, vmem, vmem),
        scratch_shapes=[
            pltpu.VMEM((8, 32, 512), BF), pltpu.VMEM((8, 32, 512), BF),
            pltpu.VMEM((1, 128), F32), pltpu.VMEM((8, 1, 128), F32),
            pltpu.VMEM((16, 16, 512), BF),
            pltpu.VMEM((8, 128), F32), pltpu.VMEM((16, 8, 128), F32),
            pltpu.VMEM((4, 16, 16, 512), BF), pltpu.VMEM((4, 8, 256), F32),
            pltpu.VMEM((1024, 512), BF), pltpu.VMEM((512, 512), BF),
            pltpu.VMEM((1024, 512), F32), pltpu.VMEM((1024, 512), BF), pltpu.VMEM((256, 512), BF),
            pltpu.VMEM((256, 512), BF), pltpu.VMEM((256, 512), BF),
            pltpu.VMEM((256, 512), BF), pltpu.VMEM((256, 512), BF),
            pltpu.VMEM((4, 64, 512), BF), pltpu.VMEM((4, 64, 512), BF),
            pltpu.VMEM((4, 64, 512), BF), pltpu.VMEM((4, 64, 512), BF),
            pltpu.VMEM((4, 16, 512), BF), pltpu.VMEM((4, 16, 512), BF),
            pltpu.VMEM((4, 16, 512), BF), pltpu.VMEM((4, 16, 512), BF),
            pltpu.VMEM((16, 1, 512), F32), pltpu.VMEM((16, 1, 512), F32),
            pltpu.VMEM((16, 1, 512), F32), pltpu.VMEM((16, 1, 512), F32),
            pltpu.VMEM((512, 512), F32), pltpu.VMEM((256, 512), F32),
            pltpu.VMEM((64, 512), F32), pltpu.VMEM((64, 512), F32),
            dma((2, 8)), dma((2, 8)), dma((2, 16)), dma((2, 16)), dma((2, 16)), dma((2, 4)),
            dma((2, 8)), dma((2, 4)), dma((2, 2)), dma((2, 8)), dma((2, 8)), dma((2, 32)),
        ],
        compiler_params=pltpu.CompilerParams(
            collective_id=0, has_side_effects=True, vmem_limit_bytes=48 * 2**20
        ),
        name="encoder_step",
    )(
        grid_lat, edge_lat, send_local.reshape(1, 128), dest_band.reshape(1, 128), receiver_in_band.reshape(1, 128),
        mesh_lat, w_edge_in, w_edge_out, w_node_in, w_node_out, norm_gain.reshape(1, 512), cotangent,
    )
    return new_mesh, grad_in, grad_out


def solution(mesh):
    in_specs = (
        P("band", None),
        P(("band", "edge"), None),
        P(("band", "edge")),
        P(("band", "edge"), None),
        P(("band", "edge")),
        P("band", None),
        P(),
        P(),
        P(None, "edge"),
        P("edge", None),
        P(),
        P("band", None),
    )
    out_specs = (P("band", None), P(("band", "edge"), None), P(("band", "edge"), None))
    return jax.shard_map(body, mesh=mesh, in_specs=in_specs, out_specs=out_specs, check_vma=False)
```

```python
import jax
import jax.numpy as jnp
from jax import lax
from jax.experimental import pallas as pl
from jax.experimental.pallas import tpu as pltpu
from jax.sharding import PartitionSpec as P

BF = jnp.bfloat16
F32 = jnp.float32
I32 = jnp.int32
MESH = pl.DeviceIdType.MESH

Z_AT = (0, 1, 15, 2, 14, 3, 13, 4, 12, 5, 11, 6, 10, 7, 9, 8)
Z_LAST = Z_AT[:0:-1]
GROUPS = ((0, 4), (4, 4), (8, 4), (12, 2), (14, 2))


def iota(shape, axis):
    return lax.broadcasted_iota(I32, shape, axis)


def one_hot(cond):
    return jnp.where(cond, 1.0, 0.0).astype(BF)


def mm(a, b):
    return jnp.dot(a, b, preferred_element_type=F32)


def mm_nt(a, b):
    return lax.dot_general(a, b, (((1,), (1,)), ((), ())), preferred_element_type=F32)


def mm_tn(a, b):
    return lax.dot_general(a, b, (((0,), (0,)), ((), ())), preferred_element_type=F32)


def sigmoid(v):
    return 0.5 * jnp.tanh(0.5 * v) + 0.5


def row_order(shape, axis, x):
    p = iota(shape, axis)
    return ((p >> 4) & 3) * 128 + (p & 15) * 8 + (p >> 6) * 4 + x


def kernel(
    grid_hbm, edge_hbm, send_hbm, dest_hbm, recv_hbm, mesh_hbm, wei_hbm, weo_hbm, wni_hbm, wno_hbm, gain_hbm, cot_hbm,
    new_hbm, gin_ref, gout_ref,
    s1_src, s1_dst, c1_src, c1_dst, z_src, r_src, xall, rx, xt, ct, wni, wno, sgrad, hid, nm,
    core_src, core_dst, y_src, y_dst, last_src, last_dst, acc,
    grid_ref, edge_ref, send_ref, dest_ref, recv_ref, mesh_ref, wei_ref, weo_ref, gain_ref, cot_ref,
    s_in, s_out, s_yc, s_yc_c, s_z, s_z_r, s_xf, s_rx, s_w, s_sh, s_core, s_y, s_last,
):
    band = lax.axis_index("band")
    x = lax.axis_index("edge")
    y, z, c = band >> 5, (band >> 1) & 15, band & 1

    def at(ty, tz, tc, tx):
        return (((ty & 3) * 16 + (tz & 15)) * 2 + (tc & 1), tx & 3)

    def copy(src, dst, sems, i, target):
        return pltpu.make_async_remote_copy(
            src_ref=src, dst_ref=dst, send_sem=sems.at[0, i], recv_sem=sems.at[1, i],
            device_id=target, device_id_type=MESH,
        )

    started, landed = [], set()

    def go(copies):
        for d in copies:
            d.start()
            started.append(d)
        return copies

    def got(copies):
        for d in copies:
            d.wait_recv()
            landed.add(id(d))

    def finish_all():
        for d in started:
            if id(d) not in landed:
                d.wait_recv()
        for d in started:
            d.wait_send()

    barrier = pltpu.get_barrier_semaphore()
    greeted = [at(y, z + i, c, x) for i in Z_AT[1:]]
    greeted += [at(y + i // 2, z, c + i % 2, x) for i in range(1, 8)]
    greeted += [at(y, z, c, x + i) for i in range(1, 4)]
    for other in greeted:
        pl.semaphore_signal(barrier, inc=1, device_id=other, device_id_type=MESH)

    lanes = pl.ds(pl.multiple_of(x * 128, 128), 128)
    half = pl.ds(pl.multiple_of(c * 512, 512), 512)

    def quarter(i):
        return pl.ds(pl.multiple_of((i & 3) * 128 + c * 64, 64), 64)

    piece = pl.ds(pl.multiple_of(c * 64, 64), 64)
    loads = {}
    for src, dst in (
        (dest_hbm, dest_ref), (send_hbm, send_ref), (recv_hbm, recv_ref), (grid_hbm, grid_ref), (edge_hbm, edge_ref),
        (wei_hbm, wei_ref), (weo_hbm, weo_ref), (wni_hbm.at[half, :], wni.at[half, lanes]),
        (wno_hbm.at[piece, :], wno.at[quarter(x), :]), (mesh_hbm, mesh_ref), (gain_hbm, gain_ref),
        (cot_hbm, cot_ref),
    ):
        i = len(loads)
        loads[i] = pltpu.make_async_copy(src, dst, s_in.at[i])
        loads[i].start()

    def loaded(*which):
        for i in which:
            loads[i].wait()

    loaded(0, 1, 2)
    eye = iota((128, 128), 0) == iota((128, 128), 1)
    dest = dest_ref[...]
    dest_b = jnp.broadcast_to(dest, (128, 128)).astype(F32)
    dest_col = jnp.sum(jnp.where(eye, dest_b, 0.0), axis=1, keepdims=True)
    earlier = (dest_col == dest_b) & (iota((128, 128), 0) < iota((128, 128), 1))
    rank = jnp.sum(jnp.where(earlier, 1.0, 0.0), axis=0, keepdims=True).astype(I32)
    slot = ((dest >> 5) * 2 + (dest & 1)) * 32 + ((dest >> 1) & 15) * 2 + rank
    code = ((dest * 2 + rank) * 256 + recv_ref[...]).astype(F32)
    send_b = jnp.broadcast_to(send_ref[...], (128, 128)).astype(F32)
    send_col = jnp.sum(jnp.where(eye, send_b, 0.0), axis=1, keepdims=True).astype(I32)
    pick = one_hot(send_col == iota((128, 1024), 1))
    loaded(3, 4)
    x_in = (mm(pick, grid_ref[...]) + edge_ref[...].astype(F32)).astype(BF)
    place = one_hot(iota((256, 128), 0) == slot)
    slots = mm(place, x_in).astype(BF)
    for i in range(8):
        s1_src[i] = slots[32 * i : 32 * (i + 1)]
    c1_src[...] = code

    pl.semaphore_wait(barrier, len(greeted))

    s1, s1_codes = [], []
    for i in (4, 5, 2, 3, 6, 7, 1):
        s1_codes.append(copy(c1_src, c1_dst.at[i], s_yc_c, i, at(y + i // 2, z, c + i % 2, x)))
    go(s1_codes)
    for i in (4, 5, 2, 3, 6, 7, 1):
        ty, tc = y + i // 2, c + i % 2
        s1.append(copy(s1_src.at[(ty & 3) * 2 + (tc & 1)], s1_dst.at[i], s_yc, i, at(ty, z, tc, x)))
    go(s1)
    weights = []
    for i in (2, 1, 3):
        target = at(y, z, c, x + i)
        weights.append(copy(wni_hbm.at[half, :], wni.at[half, lanes], s_w, i, target))
        weights.append(copy(wno_hbm.at[piece, :], wno.at[quarter(x), :], s_w, 4 + i, target))
    go(weights)
    s1_dst[0] = s1_src[y * 2 + c]
    c1_dst[0] = c1_src[...]

    o, lane = iota((256, 256), 0), iota((256, 256), 1)
    regroup = one_hot(lane == (o & 7) * 32 + (o >> 4) * 2 + ((o >> 3) & 1))
    ones = jnp.ones((128, 128), BF)
    chunk_of = one_hot(iota((16, 256), 0) == iota((16, 256), 1) >> 4)
    o, lane = iota((256, 128), 0), iota((256, 128), 1)
    in_chunk = lane == (o & 15)
    slot_code = ((((y * 16 + (o >> 4)) * 2 + c) * 2 + ((o >> 3) & 1)) * 256).astype(F32)

    got(s1_codes)
    codes = jnp.concatenate([c1_dst[i] for i in range(8)], axis=0)
    off = jnp.broadcast_to(codes[None], (32, 8, 128)).reshape(256, 128) - slot_code
    found = mm(jnp.where((off >= 0.0) & (off < 256.0), off + 1.0, 0.0).astype(BF), ones)
    found = mm(chunk_of, jnp.where(in_chunk, found, 0.0).astype(BF))
    for i in range(16):
        r_src[i] = found[i : i + 1]
    s2, s2_r = {}, {}
    for p in range(1, 16):
        i = Z_AT[p]
        s2_r[p] = copy(r_src.at[(z + i) & 15], rx.at[0, p], s_z_r, p, at(y, z + i, c, x))
        go([s2_r[p]])

    got(s1)
    gathered = mm(regroup, s1_dst[...].reshape(256, 512)).astype(BF)
    for i in range(16):
        z_src[i] = gathered[16 * i : 16 * (i + 1)]
    for p in range(1, 16):
        i = Z_AT[p]
        s2[p] = copy(z_src.at[(z + i) & 15], xall.at[0, p], s_z, p, at(y, z + i, c, x))
        go([s2[p]])
    xall[0, 0] = z_src[z]
    rx[0, 0] = r_src[z]

    loaded(5, 6)
    order = one_hot(iota((128, 512), 1) == row_order((128, 512), 0, x))

    def edge_rows(first, planes, begin, count):
        n = planes * count * 16
        rows = xall[first : first + planes, begin : begin + count].reshape(n, 512)
        z_edge = mm(rows, wei_ref[...])
        sig = sigmoid(z_edge)
        at_rows = pl.ds((begin * 4 + first * count) * 16, n)
        hid[at_rows, :] = (z_edge * sig).astype(BF)
        sgrad[at_rows, :] = sig * (1.0 + z_edge * (1.0 - sig))

    def turn_rows(begin, count):
        xt[:, begin * 64 : (begin + count) * 64] = mm_nt(
            order, xall[:, begin : begin + count].reshape(count * 64, 512)
        ).astype(BF)

    def collect(begin, count):
        n = count * 64
        rows = jnp.concatenate([rx[k, p] for k in range(4) for p in range(begin, begin + count)], axis=0)
        spread = one_hot(iota((n, 4 * count), 0) >> 4 == iota((n, 4 * count), 1))
        where = jnp.where(iota((n, 128), 1) == (iota((n, 128), 0) & 15), mm(spread, rows.astype(BF)), 0.0)
        where = mm(where.astype(BF), jnp.ones((128, 256), BF))
        hit = one_hot(where == (iota((n, 256), 1) + 1).astype(F32))
        ct[begin * 64 : begin * 64 + n, :] = hit
        return mm_tn(hit, hid[begin * 64 : begin * 64 + n, :])

    forward = []
    for begin, count in GROUPS:
        new = [p for p in range(begin, begin + count) if p]
        got([s2[p] for p in new])
        got([s2_r[p] for p in new])
        part = pl.ds(begin, count)
        sent = [copy(xall.at[0, part], xall.at[i, part], s_xf, begin * 4 + i, at(y, z, c, x + i)) for i in (2, 1, 3)]
        sent += [copy(rx.at[0, part], rx.at[i, part], s_rx, begin * 4 + i, at(y, z, c, x + i)) for i in (2, 1, 3)]
        forward.append(go(sent))
        edge_rows(0, 1, begin, count)
        if begin == GROUPS[1][0]:
            got(weights)
            loaded(7, 8)
            other = at(y, z, c + 1, x)
            shared = [copy(wni.at[half, :], wni.at[half, :], s_sh, 0, other)]
            for i in range(4):
                shared.append(copy(wno.at[quarter(i), :], wno.at[quarter(i), :], s_sh, 1 + i, other))
            go(shared)
        if begin == GROUPS[3][0]:
            got(shared)
            loaded(9, 10, 11)
            mesh = mesh_ref[...]
            z_mesh = mm(mesh, wni[0:512, :])
            w_both = mm_tn(weo_ref[...], wni[512:1024, :]).astype(BF)
            w_turn = mm(order, wni[512:1024, :]).astype(BF)

    agg_h = jnp.zeros((256, 512), F32)
    for (begin, count), sent in zip(GROUPS, forward):
        got(sent)
        edge_rows(1, 3, begin, count)
        agg_h += collect(begin, count)
        if begin < GROUPS[-1][0]:
            turn_rows(begin, count)

    agg_h = agg_h.astype(BF)
    z_node = z_mesh + mm(agg_h, w_both)
    sig = sigmoid(z_node)
    h_node = (z_node * sig).astype(BF)
    y_out = mm(h_node, wno[...])
    gain = gain_ref[...]
    mean_y = jnp.mean(y_out, axis=1, keepdims=True)
    centred = y_out - mean_y
    inv_std = lax.rsqrt(jnp.mean(centred * centred, axis=1, keepdims=True) + 1e-05)
    normed = centred * inv_std
    up = cot_ref[...].astype(F32) * gain
    d_y = (
        up - jnp.mean(up, axis=1, keepdims=True) - normed * jnp.mean(up * normed, axis=1, keepdims=True)
    ) * inv_std
    dh_node = mm_nt(d_y.astype(BF), wno[...])
    dz_node = (dh_node * (sig * (1.0 + z_node * (1.0 - sig)))).astype(BF)
    dh = mm_nt(dz_node, w_both).astype(BF)
    d_agg = mm_nt(dz_node, w_turn).astype(BF)

    turn_rows(*GROUPS[-1])
    d_edge = (mm(ct[...], dh) * sgrad[...]).astype(BF)
    acc[0] = mm(xt[...], d_edge)
    acc[1] = mm_tn(d_agg, agg_h)
    keep = pl.ds(pl.multiple_of(c * 64, 64), 64)
    give = pl.ds(pl.multiple_of((1 - c) * 64, 64), 64)
    core_src[...] = acc[:, give, :].astype(BF)
    to_core = go([copy(core_src, core_dst, s_core, 0, other)])
    nm[...] = (mesh.astype(F32) + normed * gain).astype(BF)
    stored = pltpu.make_async_copy(nm, new_hbm, s_out)
    stored.start()

    got(to_core)
    acc[:, keep, :] += core_dst[...].astype(F32)
    for i in range(4):
        y_src[i] = acc[:, pl.ds(pl.multiple_of(c * 64 + i * 16, 16), 16), :].astype(BF)
    to_y = go([copy(y_src.at[(y + i) & 3], y_dst.at[i], s_y, i, at(y + i, z, c, x)) for i in (2, 1, 3)])
    got(to_y)
    rows = acc[:, pl.ds(pl.multiple_of(c * 64 + y * 16, 16), 16), :]
    for i in range(1, 4):
        rows += y_dst[i].astype(F32)
    for i in range(16):
        last_src[i, 0] = rows[0, i : i + 1]
        last_src[i, 1] = rows[1, i : i + 1]
    to_z = []
    for i in Z_LAST:
        to_z += go([copy(last_src.at[(z + i) & 15], last_dst.at[i], s_last, i, at(y, z + i, c, x))])
    total = last_src[z]
    for i in Z_AT[1:]:
        got([to_z[Z_LAST.index(i)]])
        total += last_dst[i]
    gin_ref[...] = total[0]
    gout_ref[...] = total[1]
    stored.wait()
    finish_all()


def body(
    grid_lat, edge_lat, send_local, dest_band, receiver_in_band, mesh_lat,
    w_edge_in, w_edge_out, w_node_in, w_node_out, norm_gain, cotangent,
):
    vmem = pl.BlockSpec(memory_space=pltpu.VMEM)
    dma = pltpu.SemaphoreType.DMA
    new_mesh, grad_in, grad_out = pl.pallas_call(
        kernel,
        out_shape=(
            jax.ShapeDtypeStruct((256, 512), BF),
            jax.ShapeDtypeStruct((1, 512), F32),
            jax.ShapeDtypeStruct((1, 512), F32),
        ),
        in_specs=[pl.BlockSpec(memory_space=pl.ANY)] * 12,
        out_specs=(pl.BlockSpec(memory_space=pl.ANY), vmem, vmem),
        scratch_shapes=[
            pltpu.VMEM((8, 32, 512), BF), pltpu.VMEM((8, 32, 512), BF),
            pltpu.VMEM((1, 128), F32), pltpu.VMEM((8, 1, 128), F32),
            pltpu.VMEM((16, 16, 512), BF), pltpu.VMEM((16, 1, 128), F32),
            pltpu.VMEM((4, 16, 16, 512), BF), pltpu.VMEM((4, 16, 1, 128), F32),
            pltpu.VMEM((128, 1024), BF), pltpu.VMEM((1024, 256), BF),
            pltpu.VMEM((1024, 512), BF), pltpu.VMEM((512, 512), BF),
            pltpu.VMEM((1024, 512), F32), pltpu.VMEM((1024, 512), BF), pltpu.VMEM((256, 512), BF),
            pltpu.VMEM((2, 64, 512), BF), pltpu.VMEM((2, 64, 512), BF),
            pltpu.VMEM((4, 2, 16, 512), BF), pltpu.VMEM((4, 2, 16, 512), BF),
            pltpu.VMEM((16, 2, 1, 512), F32), pltpu.VMEM((16, 2, 1, 512), F32), pltpu.VMEM((2, 128, 512), F32),
            pltpu.VMEM((1024, 512), BF), pltpu.VMEM((128, 512), BF),
            pltpu.VMEM((1, 128), I32), pltpu.VMEM((1, 128), I32), pltpu.VMEM((1, 128), I32),
            pltpu.VMEM((256, 512), BF), pltpu.VMEM((512, 512), BF), pltpu.VMEM((512, 512), BF),
            pltpu.VMEM((1, 512), F32), pltpu.VMEM((256, 512), BF),
            dma((12,)), dma, dma((2, 8)), dma((2, 8)), dma((2, 16)), dma((2, 16)), dma((2, 64)), dma((2, 64)),
            dma((2, 8)), dma((2, 5)), dma((2, 1)), dma((2, 4)), dma((2, 16)),
        ],
        compiler_params=pltpu.CompilerParams(
            collective_id=0, has_side_effects=True, vmem_limit_bytes=56 * 2**20
        ),
        name="encoder_step",
    )(
        grid_lat, edge_lat, send_local.reshape(1, 128), dest_band.reshape(1, 128), receiver_in_band.reshape(1, 128),
        mesh_lat, w_edge_in, w_edge_out, w_node_in, w_node_out, norm_gain.reshape(1, 512), cotangent,
    )
    return new_mesh, grad_in, grad_out


def solution(mesh):
    in_specs = (
        P("band", None),
        P(("band", "edge"), None),
        P(("band", "edge")),
        P(("band", "edge"), None),
        P(("band", "edge")),
        P("band", None),
        P(),
        P(),
        P(None, "edge"),
        P("edge", None),
        P(),
        P("band", None),
    )
    out_specs = (P("band", None), P(("band", "edge"), None), P(("band", "edge"), None))
    return jax.shard_map(body, mesh=mesh, in_specs=in_specs, out_specs=out_specs, check_vma=False)
```

```python
import jax
import jax.numpy as jnp
from jax import lax
from jax.experimental import pallas as pl
from jax.experimental.pallas import tpu as pltpu
from jax.sharding import PartitionSpec as P

BF = jnp.bfloat16
F32 = jnp.float32
I32 = jnp.int32
MESH = pl.DeviceIdType.MESH

Z_AT = (0, 1, 15, 2, 14, 3, 13, 4, 12, 5, 11, 6, 10, 7, 9, 8)
Z_LAST = Z_AT[:0:-1]
GROUPS = ((0, 4), (4, 4), (8, 2), (10, 2), (12, 2), (14, 2))


def iota(shape, axis):
    return lax.broadcasted_iota(I32, shape, axis)


def one_hot(cond):
    return jnp.where(cond, 1.0, 0.0).astype(BF)


def mm(a, b):
    return jnp.dot(a, b, preferred_element_type=F32)


def mm_nt(a, b):
    return lax.dot_general(a, b, (((1,), (1,)), ((), ())), preferred_element_type=F32)


def mm_tn(a, b):
    return lax.dot_general(a, b, (((0,), (0,)), ((), ())), preferred_element_type=F32)


def sigmoid(v):
    return 0.5 * jnp.tanh(0.5 * v) + 0.5


def row_order(shape, axis, x):
    p = iota(shape, axis)
    return ((p >> 4) & 3) * 128 + (p & 15) * 8 + (p >> 6) * 4 + x


def kernel(
    grid_hbm, edge_hbm, send_hbm, dest_hbm, recv_hbm, mesh_hbm, wei_hbm, weo_hbm, wni_hbm, wno_hbm, gain_hbm, cot_hbm,
    new_hbm, gin_ref, gout_ref,
    s1_src, s1_dst, c1_src, c1_dst, z_src, r_src, xall, rx, xt, ct, wni, wno, sgrad, hid, nm,
    core_src, core_dst, y_src, y_dst, last_src, last_dst, acc,
    grid_ref, edge_ref, send_ref, dest_ref, recv_ref, mesh_ref, wei_ref, weo_ref, gain_ref, cot_ref,
    s_in, s_out, s_yc, s_yc_c, s_z, s_z_r, s_xf, s_rx, s_w, s_sh, s_core, s_y, s_last,
):
    band = lax.axis_index("band")
    x = lax.axis_index("edge")
    y, z, c = band >> 5, (band >> 1) & 15, band & 1

    def at(ty, tz, tc, tx):
        return (((ty & 3) * 16 + (tz & 15)) * 2 + (tc & 1), tx & 3)

    def copy(src, dst, sems, i, target):
        return pltpu.make_async_remote_copy(
            src_ref=src, dst_ref=dst, send_sem=sems.at[0, i], recv_sem=sems.at[1, i],
            device_id=target, device_id_type=MESH,
        )

    started, landed = [], set()

    def go(copies):
        for d in copies:
            d.start()
            started.append(d)
        return copies

    def got(copies):
        for d in copies:
            d.wait_recv()
            landed.add(id(d))

    def finish_all():
        for d in started:
            if id(d) not in landed:
                d.wait_recv()
        for d in started:
            d.wait_send()

    barrier = pltpu.get_barrier_semaphore()
    greeted = [at(y, z + i, c, x) for i in Z_LAST]
    greeted += [at(y + i // 2, z, c + i % 2, x) for i in range(1, 8)]
    greeted += [at(y, z, c, x + i) for i in range(1, 4)]
    for other in greeted:
        pl.semaphore_signal(barrier, inc=1, device_id=other, device_id_type=MESH)

    lanes = pl.ds(pl.multiple_of(x * 128, 128), 128)
    half = pl.ds(pl.multiple_of(c * 512, 512), 512)

    def quarter(i):
        return pl.ds(pl.multiple_of((i & 3) * 128 + c * 64, 64), 64)

    piece = pl.ds(pl.multiple_of(c * 64, 64), 64)
    loads = {}
    for src, dst in (
        (dest_hbm, dest_ref), (send_hbm, send_ref), (recv_hbm, recv_ref), (grid_hbm, grid_ref), (edge_hbm, edge_ref),
        (wei_hbm, wei_ref), (weo_hbm, weo_ref), (wni_hbm.at[half, :], wni.at[half, lanes]),
        (wno_hbm.at[piece, :], wno.at[quarter(x), :]), (mesh_hbm, mesh_ref), (gain_hbm, gain_ref),
        (cot_hbm, cot_ref),
    ):
        i = len(loads)
        loads[i] = pltpu.make_async_copy(src, dst, s_in.at[i])
        loads[i].start()

    def loaded(*which):
        for i in which:
            loads[i].wait()

    loaded(0, 1, 2)
    eye = iota((128, 128), 0) == iota((128, 128), 1)
    dest = dest_ref[...]
    dest_b = jnp.broadcast_to(dest, (128, 128)).astype(F32)
    dest_col = jnp.sum(jnp.where(eye, dest_b, 0.0), axis=1, keepdims=True)
    earlier = (dest_col == dest_b) & (iota((128, 128), 0) < iota((128, 128), 1))
    rank = jnp.sum(jnp.where(earlier, 1.0, 0.0), axis=0, keepdims=True).astype(I32)
    slot = ((dest >> 5) * 2 + (dest & 1)) * 32 + ((dest >> 1) & 15) * 2 + rank
    code = ((dest * 2 + rank) * 256 + recv_ref[...]).astype(F32)
    send_b = jnp.broadcast_to(send_ref[...], (128, 128)).astype(F32)
    send_col = jnp.sum(jnp.where(eye, send_b, 0.0), axis=1, keepdims=True).astype(I32)
    pick = one_hot(send_col == iota((128, 1024), 1))
    loaded(3, 4)
    x_in = (mm(pick, grid_ref[...]) + edge_ref[...].astype(F32)).astype(BF)
    place = one_hot(iota((256, 128), 0) == slot)
    slots = mm(place, x_in).astype(BF)
    for i in range(8):
        s1_src[i] = slots[32 * i : 32 * (i + 1)]
    c1_src[...] = code

    pl.semaphore_wait(barrier, len(greeted))

    s1, s1_codes = [], []
    for i in (4, 5, 2, 3, 6, 7, 1):
        s1_codes.append(copy(c1_src, c1_dst.at[i], s_yc_c, i, at(y + i // 2, z, c + i % 2, x)))
    go(s1_codes)
    for i in (4, 5, 2, 3, 6, 7, 1):
        ty, tc = y + i // 2, c + i % 2
        s1.append(copy(s1_src.at[(ty & 3) * 2 + (tc & 1)], s1_dst.at[i], s_yc, i, at(ty, z, tc, x)))
    go(s1)
    weights = []
    for i in (2, 1, 3):
        target = at(y, z, c, x + i)
        weights.append(copy(wni_hbm.at[half, :], wni.at[half, lanes], s_w, i, target))
        weights.append(copy(wno_hbm.at[piece, :], wno.at[quarter(x), :], s_w, 4 + i, target))
    go(weights)
    s1_dst[0] = s1_src[y * 2 + c]
    c1_dst[0] = c1_src[...]

    o, lane = iota((256, 256), 0), iota((256, 256), 1)
    regroup = one_hot(lane == (o & 7) * 32 + (o >> 4) * 2 + ((o >> 3) & 1))
    ones = jnp.ones((128, 128), BF)
    chunk_of = one_hot(iota((16, 256), 0) == iota((16, 256), 1) >> 4)
    o, lane = iota((256, 128), 0), iota((256, 128), 1)
    in_chunk = lane == (o & 15)
    slot_code = ((((y * 16 + (o >> 4)) * 2 + c) * 2 + ((o >> 3) & 1)) * 256).astype(F32)

    got(s1_codes)
    codes = jnp.concatenate([c1_dst[i] for i in range(8)], axis=0)
    off = jnp.broadcast_to(codes[None], (32, 8, 128)).reshape(256, 128) - slot_code
    found = mm(jnp.where((off >= 0.0) & (off < 256.0), off + 1.0, 0.0).astype(BF), ones)
    found = mm(chunk_of, jnp.where(in_chunk, found, 0.0).astype(BF))
    for i in range(16):
        r_src[i] = found[i : i + 1]
    s2, s2_r = {}, {}
    for p in range(1, 16):
        i = Z_AT[p]
        s2_r[p] = copy(r_src.at[(z + i) & 15], rx.at[0, p], s_z_r, p, at(y, z + i, c, x))
        go([s2_r[p]])

    got(s1)
    gathered = mm(regroup, s1_dst[...].reshape(256, 512)).astype(BF)
    for i in range(16):
        z_src[i] = gathered[16 * i : 16 * (i + 1)]
    for p in range(1, 16):
        i = Z_AT[p]
        s2[p] = copy(z_src.at[(z + i) & 15], xall.at[0, p], s_z, p, at(y, z + i, c, x))
        go([s2[p]])
    xall[0, 0] = z_src[z]
    rx[0, 0] = r_src[z]

    loaded(5, 6)
    order = one_hot(iota((128, 512), 1) == row_order((128, 512), 0, x))

    def edge_rows(first, planes, begin, count):
        n = planes * count * 16
        rows = xall[first : first + planes, begin : begin + count].reshape(n, 512)
        z_edge = mm(rows, wei_ref[...])
        sig = sigmoid(z_edge)
        at_rows = pl.ds((begin * 4 + first * count) * 16, n)
        hid[at_rows, :] = (z_edge * sig).astype(BF)
        sgrad[at_rows, :] = sig * (1.0 + z_edge * (1.0 - sig))

    def turn_rows(begin, count):
        xt[:, begin * 64 : (begin + count) * 64] = mm_nt(
            order, xall[:, begin : begin + count].reshape(count * 64, 512)
        ).astype(BF)

    def collect(begin, count):
        n = count * 64
        rows = jnp.concatenate([rx[k, p] for k in range(4) for p in range(begin, begin + count)], axis=0)
        spread = one_hot(iota((n, 4 * count), 0) >> 4 == iota((n, 4 * count), 1))
        where = jnp.where(iota((n, 128), 1) == (iota((n, 128), 0) & 15), mm(spread, rows.astype(BF)), 0.0)
        where = mm(where.astype(BF), jnp.ones((128, 256), BF))
        hit = one_hot(where == (iota((n, 256), 1) + 1).astype(F32))
        ct[begin * 64 : begin * 64 + n, :] = hit
        return mm_tn(hit, hid[begin * 64 : begin * 64 + n, :])

    forward = []
    for begin, count in GROUPS:
        new = [p for p in range(begin, begin + count) if p]
        got([s2[p] for p in new])
        got([s2_r[p] for p in new])
        part = pl.ds(begin, count)
        sent = [copy(xall.at[0, part], xall.at[i, part], s_xf, begin * 4 + i, at(y, z, c, x + i)) for i in (2, 1, 3)]
        sent += [copy(rx.at[0, part], rx.at[i, part], s_rx, begin * 4 + i, at(y, z, c, x + i)) for i in (2, 1, 3)]
        forward.append(go(sent))
        edge_rows(0, 1, begin, count)
        if begin == GROUPS[1][0]:
            got(weights)
            loaded(7, 8)
            other = at(y, z, c + 1, x)
            shared = [copy(wni.at[half, :], wni.at[half, :], s_sh, 0, other)]
            for i in range(4):
                shared.append(copy(wno.at[quarter(i), :], wno.at[quarter(i), :], s_sh, 1 + i, other))
            go(shared)
        if begin == GROUPS[3][0]:
            got(shared)
            loaded(9, 10, 11)
            mesh = mesh_ref[...]
            z_mesh = mm(mesh, wni[0:512, :])
            w_both = mm_tn(weo_ref[...], wni[512:1024, :]).astype(BF)
            w_turn = mm(order, wni[512:1024, :]).astype(BF)
            w_last = wno[...].astype(F32)
            w_flat = (w_last - jnp.mean(w_last, axis=1, keepdims=True)).astype(BF)
            gain = gain_ref[...]
            up = cot_ref[...].astype(F32) * gain
            up = up - jnp.mean(up, axis=1, keepdims=True)

    agg_h = jnp.zeros((256, 512), F32)
    for (begin, count), sent in zip(GROUPS, forward):
        got(sent)
        edge_rows(1, 3, begin, count)
        agg_h += collect(begin, count)
        if begin < GROUPS[-1][0]:
            turn_rows(begin, count)

    agg_h = agg_h.astype(BF)
    halves = (slice(0, 128), slice(128, 256))
    z_node = [z_mesh[h] + mm(agg_h[h], w_both) for h in halves]
    sig = [sigmoid(v) for v in z_node]
    h_node = [(v * s).astype(BF) for v, s in zip(z_node, sig)]
    centred = [mm(v, w_flat) for v in h_node]
    inv_std = [lax.rsqrt(jnp.mean(v * v, axis=1, keepdims=True) + 1e-05) for v in centred]
    normed = [v * s for v, s in zip(centred, inv_std)]
    d_y = [
        ((up[h] - v * jnp.mean(up[h] * v, axis=1, keepdims=True)) * s).astype(BF)
        for h, v, s in zip(halves, normed, inv_std)
    ]
    dz_node = [
        (mm_nt(d, wno[...]) * (s * (1.0 + v * (1.0 - s)))).astype(BF) for d, s, v in zip(d_y, sig, z_node)
    ]
    dh = jnp.concatenate([mm_nt(d, w_both).astype(BF) for d in dz_node], axis=0)
    d_agg = jnp.concatenate([mm_nt(d, w_turn).astype(BF) for d in dz_node], axis=0)

    turn_rows(*GROUPS[-1])
    d_edge = (mm(ct[...], dh) * sgrad[...]).astype(BF)
    acc[0] = mm(xt[...], d_edge)
    acc[1] = mm_tn(d_agg, agg_h)
    keep = pl.ds(pl.multiple_of(c * 64, 64), 64)
    give = pl.ds(pl.multiple_of((1 - c) * 64, 64), 64)
    core_src[...] = acc[:, give, :].astype(BF)
    to_core = go([copy(core_src, core_dst, s_core, 0, other)])
    for h, v in zip(halves, normed):
        nm[h, :] = (mesh[h].astype(F32) + v * gain).astype(BF)
    stored = pltpu.make_async_copy(nm, new_hbm, s_out)
    stored.start()

    got(to_core)
    acc[:, keep, :] += core_dst[...].astype(F32)
    for i in range(4):
        y_src[i] = acc[:, pl.ds(pl.multiple_of(c * 64 + i * 16, 16), 16), :].astype(BF)
    to_y = go([copy(y_src.at[(y + i) & 3], y_dst.at[i], s_y, i, at(y + i, z, c, x)) for i in (2, 1, 3)])
    got(to_y)
    rows = acc[:, pl.ds(pl.multiple_of(c * 64 + y * 16, 16), 16), :]
    for i in range(1, 4):
        rows += y_dst[i].astype(F32)
    for i in range(16):
        last_src[i, 0] = rows[0, i : i + 1]
        last_src[i, 1] = rows[1, i : i + 1]
    to_z = []
    for i in Z_LAST:
        to_z += go([copy(last_src.at[(z + i) & 15], last_dst.at[i], s_last, i, at(y, z + i, c, x))])
    total = last_src[z]
    for i in Z_AT[1:]:
        got([to_z[Z_LAST.index(i)]])
        total += last_dst[i]
    gin_ref[...] = total[0]
    gout_ref[...] = total[1]
    stored.wait()
    finish_all()


def body(
    grid_lat, edge_lat, send_local, dest_band, receiver_in_band, mesh_lat,
    w_edge_in, w_edge_out, w_node_in, w_node_out, norm_gain, cotangent,
):
    vmem = pl.BlockSpec(memory_space=pltpu.VMEM)
    dma = pltpu.SemaphoreType.DMA
    new_mesh, grad_in, grad_out = pl.pallas_call(
        kernel,
        out_shape=(
            jax.ShapeDtypeStruct((256, 512), BF),
            jax.ShapeDtypeStruct((1, 512), F32),
            jax.ShapeDtypeStruct((1, 512), F32),
        ),
        in_specs=[pl.BlockSpec(memory_space=pl.ANY)] * 12,
        out_specs=(pl.BlockSpec(memory_space=pl.ANY), vmem, vmem),
        scratch_shapes=[
            pltpu.VMEM((8, 32, 512), BF), pltpu.VMEM((8, 32, 512), BF),
            pltpu.VMEM((1, 128), F32), pltpu.VMEM((8, 1, 128), F32),
            pltpu.VMEM((16, 16, 512), BF), pltpu.VMEM((16, 1, 128), F32),
            pltpu.VMEM((4, 16, 16, 512), BF), pltpu.VMEM((4, 16, 1, 128), F32),
            pltpu.VMEM((128, 1024), BF), pltpu.VMEM((1024, 256), BF),
            pltpu.VMEM((1024, 512), BF), pltpu.VMEM((512, 512), BF),
            pltpu.VMEM((1024, 512), F32), pltpu.VMEM((1024, 512), BF), pltpu.VMEM((256, 512), BF),
            pltpu.VMEM((2, 64, 512), BF), pltpu.VMEM((2, 64, 512), BF),
            pltpu.VMEM((4, 2, 16, 512), BF), pltpu.VMEM((4, 2, 16, 512), BF),
            pltpu.VMEM((16, 2, 1, 512), F32), pltpu.VMEM((16, 2, 1, 512), F32), pltpu.VMEM((2, 128, 512), F32),
            pltpu.VMEM((1024, 512), BF), pltpu.VMEM((128, 512), BF),
            pltpu.VMEM((1, 128), I32), pltpu.VMEM((1, 128), I32), pltpu.VMEM((1, 128), I32),
            pltpu.VMEM((256, 512), BF), pltpu.VMEM((512, 512), BF), pltpu.VMEM((512, 512), BF),
            pltpu.VMEM((1, 512), F32), pltpu.VMEM((256, 512), BF),
            dma((12,)), dma, dma((2, 8)), dma((2, 8)), dma((2, 16)), dma((2, 16)), dma((2, 64)), dma((2, 64)),
            dma((2, 8)), dma((2, 5)), dma((2, 1)), dma((2, 4)), dma((2, 16)),
        ],
        compiler_params=pltpu.CompilerParams(
            collective_id=0, has_side_effects=True, vmem_limit_bytes=56 * 2**20
        ),
        name="encoder_step",
    )(
        grid_lat, edge_lat, send_local.reshape(1, 128), dest_band.reshape(1, 128), receiver_in_band.reshape(1, 128),
        mesh_lat, w_edge_in, w_edge_out, w_node_in, w_node_out, norm_gain.reshape(1, 512), cotangent,
    )
    return new_mesh, grad_in, grad_out


def solution(mesh):
    in_specs = (
        P("band", None),
        P(("band", "edge"), None),
        P(("band", "edge")),
        P(("band", "edge"), None),
        P(("band", "edge")),
        P("band", None),
        P(),
        P(),
        P(None, "edge"),
        P("edge", None),
        P(),
        P("band", None),
    )
    out_specs = (P("band", None), P(("band", "edge"), None), P(("band", "edge"), None))
    return jax.shard_map(body, mesh=mesh, in_specs=in_specs, out_specs=out_specs, check_vma=False)
```

```python
import jax
import jax.numpy as jnp
from jax import lax
from jax.experimental import pallas as pl
from jax.experimental.pallas import tpu as pltpu
from jax.sharding import PartitionSpec as P

BF = jnp.bfloat16
F32 = jnp.float32
I32 = jnp.int32
MESH = pl.DeviceIdType.MESH

Z_AT = (0, 1, 15, 2, 14, 3, 13, 4, 12, 5, 11, 6, 10, 7, 9, 8)
Z_LAST = Z_AT[:0:-1]
GROUPS = ((0, 4), (4, 4), (8, 2), (10, 2), (12, 2), (14, 2))


LAG = 3


def iota(shape, axis):
    return lax.broadcasted_iota(I32, shape, axis)


def one_hot(cond):
    return jnp.where(cond, 1.0, 0.0).astype(BF)


def mm(a, b):
    return jnp.dot(a, b, preferred_element_type=F32)


def mm_nt(a, b):
    return lax.dot_general(a, b, (((1,), (1,)), ((), ())), preferred_element_type=F32)


def mm_tn(a, b):
    return lax.dot_general(a, b, (((0,), (0,)), ((), ())), preferred_element_type=F32)


def sigmoid(v):
    return 0.5 * jnp.tanh(0.5 * v) + 0.5


def row_order(shape, axis, x):
    p = iota(shape, axis)
    return ((p >> 4) & 3) * 128 + (p & 15) * 8 + (p >> 6) * 4 + x


def kernel(
    grid_hbm, edge_hbm, send_hbm, dest_hbm, recv_hbm, mesh_hbm, wei_hbm, weo_hbm, wni_hbm, wno_hbm, gain_hbm, cot_hbm,
    new_hbm, gin_ref, gout_ref,
    s1_src, s1_dst, c1_src, c1_dst, z_src, r_src, xall, rx, xt, ct, wni, wno, sgrad, hid, nm,
    core_src, core_dst, y_src, y_dst, last_src, last_dst, acc,
    grid_ref, edge_ref, send_ref, dest_ref, recv_ref, mesh_ref, wei_ref, weo_ref, gain_ref, cot_ref,
    s_in, s_out, s_yc, s_yc_c, s_z, s_z_r, s_xf, s_rx, s_w, s_sh, s_core, s_y, s_last,
):
    band = lax.axis_index("band")
    x = lax.axis_index("edge")
    y, z, c = band >> 5, (band >> 1) & 15, band & 1

    def at(ty, tz, tc, tx):
        return (((ty & 3) * 16 + (tz & 15)) * 2 + (tc & 1), tx & 3)

    def copy(src, dst, sems, i, target):
        return pltpu.make_async_remote_copy(
            src_ref=src, dst_ref=dst, send_sem=sems.at[0, i], recv_sem=sems.at[1, i],
            device_id=target, device_id_type=MESH,
        )

    started, landed = [], set()

    def go(copies):
        for d in copies:
            d.start()
            started.append(d)
        return copies

    def got(copies):
        for d in copies:
            d.wait_recv()
            landed.add(id(d))

    def finish_all():
        for d in started:
            if id(d) not in landed:
                d.wait_recv()
        for d in started:
            d.wait_send()

    barrier = pltpu.get_barrier_semaphore()
    greeted = [at(y, z + i, c, x) for i in Z_LAST]
    greeted += [at(y + i // 2, z, c + i % 2, x) for i in range(1, 8)]
    greeted += [at(y, z, c, x + i) for i in range(1, 4)]
    for other in greeted:
        pl.semaphore_signal(barrier, inc=1, device_id=other, device_id_type=MESH)

    lanes = pl.ds(pl.multiple_of(x * 128, 128), 128)
    half = pl.ds(pl.multiple_of(c * 512, 512), 512)

    def quarter(i):
        return pl.ds(pl.multiple_of((i & 3) * 128 + c * 64, 64), 64)

    piece = pl.ds(pl.multiple_of(c * 64, 64), 64)
    loads = {}
    for src, dst in (
        (dest_hbm, dest_ref), (send_hbm, send_ref), (recv_hbm, recv_ref), (grid_hbm, grid_ref), (edge_hbm, edge_ref),
        (wei_hbm, wei_ref), (weo_hbm, weo_ref), (wni_hbm.at[half, :], wni.at[half, lanes]),
        (wno_hbm.at[piece, :], wno.at[quarter(x), :]), (mesh_hbm, mesh_ref), (gain_hbm, gain_ref),
        (cot_hbm, cot_ref),
    ):
        i = len(loads)
        loads[i] = pltpu.make_async_copy(src, dst, s_in.at[i])
        loads[i].start()

    def loaded(*which):
        for i in which:
            loads[i].wait()

    loaded(0, 1, 2)
    eye = iota((128, 128), 0) == iota((128, 128), 1)
    dest = dest_ref[...]
    dest_b = jnp.broadcast_to(dest, (128, 128)).astype(F32)
    dest_col = jnp.sum(jnp.where(eye, dest_b, 0.0), axis=1, keepdims=True)
    earlier = (dest_col == dest_b) & (iota((128, 128), 0) < iota((128, 128), 1))
    rank = jnp.sum(jnp.where(earlier, 1.0, 0.0), axis=0, keepdims=True).astype(I32)
    slot = ((dest >> 5) * 2 + (dest & 1)) * 32 + ((dest >> 1) & 15) * 2 + rank
    code = ((dest * 2 + rank) * 256 + recv_ref[...]).astype(F32)
    send_b = jnp.broadcast_to(send_ref[...], (128, 128)).astype(F32)
    send_col = jnp.sum(jnp.where(eye, send_b, 0.0), axis=1, keepdims=True).astype(I32)
    pick = one_hot(send_col == iota((128, 1024), 1))
    loaded(3, 4)
    x_in = (mm(pick, grid_ref[...]) + edge_ref[...].astype(F32)).astype(BF)
    place = one_hot(iota((256, 128), 0) == slot)
    slots = mm(place, x_in).astype(BF)
    for i in range(8):
        s1_src[i] = slots[32 * i : 32 * (i + 1)]
    c1_src[...] = code

    pl.semaphore_wait(barrier, len(greeted))

    s1, s1_codes = [], []
    for i in (4, 5, 2, 3, 6, 7, 1):
        s1_codes.append(copy(c1_src, c1_dst.at[i], s_yc_c, i, at(y + i // 2, z, c + i % 2, x)))
    go(s1_codes)
    for i in (4, 5, 2, 3, 6, 7, 1):
        ty, tc = y + i // 2, c + i % 2
        s1.append(copy(s1_src.at[(ty & 3) * 2 + (tc & 1)], s1_dst.at[i], s_yc, i, at(ty, z, tc, x)))
    go(s1)
    weights = []
    for i in (2, 1, 3):
        target = at(y, z, c, x + i)
        weights.append(copy(wni_hbm.at[half, :], wni.at[half, lanes], s_w, i, target))
        weights.append(copy(wno_hbm.at[piece, :], wno.at[quarter(x), :], s_w, 4 + i, target))
    go(weights)
    s1_dst[0] = s1_src[y * 2 + c]
    c1_dst[0] = c1_src[...]

    o, lane = iota((256, 256), 0), iota((256, 256), 1)
    regroup = one_hot(lane == (o & 7) * 32 + (o >> 4) * 2 + ((o >> 3) & 1))
    ones = jnp.ones((128, 128), BF)
    chunk_of = one_hot(iota((16, 256), 0) == iota((16, 256), 1) >> 4)
    o, lane = iota((256, 128), 0), iota((256, 128), 1)
    in_chunk = lane == (o & 15)
    slot_code = ((((y * 16 + (o >> 4)) * 2 + c) * 2 + ((o >> 3) & 1)) * 256).astype(F32)

    got(s1_codes)
    codes = jnp.concatenate([c1_dst[i] for i in range(8)], axis=0)
    off = jnp.broadcast_to(codes[None], (32, 8, 128)).reshape(256, 128) - slot_code
    found = mm(jnp.where((off >= 0.0) & (off < 256.0), off + 1.0, 0.0).astype(BF), ones)
    found = mm(chunk_of, jnp.where(in_chunk, found, 0.0).astype(BF))
    for i in range(16):
        r_src[i] = found[i : i + 1]
    s2, s2_r = {}, {}
    for p in range(1, 16):
        i = Z_AT[p]
        s2_r[p] = copy(r_src.at[(z + i) & 15], rx.at[0, p], s_z_r, p, at(y, z + i, c, x))
        go([s2_r[p]])

    got(s1)
    gathered = mm(regroup, s1_dst[...].reshape(256, 512)).astype(BF)
    for i in range(16):
        z_src[i] = gathered[16 * i : 16 * (i + 1)]
    for p in range(1, 16):
        i = Z_AT[p]
        s2[p] = copy(z_src.at[(z + i) & 15], xall.at[0, p], s_z, p, at(y, z + i, c, x))
        go([s2[p]])
    xall[0, 0] = z_src[z]
    rx[0, 0] = r_src[z]

    loaded(5, 6)
    order = one_hot(iota((128, 512), 1) == row_order((128, 512), 0, x))

    def edge_rows(first, planes, begin, count):
        n = planes * count * 16
        rows = xall[first : first + planes, begin : begin + count].reshape(n, 512)
        z_edge = mm(rows, wei_ref[...])
        sig = sigmoid(z_edge)
        at_rows = pl.ds((begin * 4 + first * count) * 16, n)
        hid[at_rows, :] = (z_edge * sig).astype(BF)
        sgrad[at_rows, :] = sig * (1.0 + z_edge * (1.0 - sig))

    def turn_rows(begin, count):
        xt[:, begin * 64 : (begin + count) * 64] = mm_nt(
            order, xall[:, begin : begin + count].reshape(count * 64, 512)
        ).astype(BF)

    def collect(begin, count):
        n = count * 64
        rows = jnp.concatenate([rx[k, p] for k in range(4) for p in range(begin, begin + count)], axis=0)
        spread = one_hot(iota((n, 4 * count), 0) >> 4 == iota((n, 4 * count), 1))
        where = jnp.where(iota((n, 128), 1) == (iota((n, 128), 0) & 15), mm(spread, rows.astype(BF)), 0.0)
        where = mm(where.astype(BF), jnp.ones((128, 256), BF))
        hit = one_hot(where == (iota((n, 256), 1) + 1).astype(F32))
        ct[begin * 64 : begin * 64 + n, :] = hit
        return mm_tn(hit, hid[begin * 64 : begin * 64 + n, :])

    def whole_group(k):
        begin, count = GROUPS[k]
        got(forward[k])
        edge_rows(1, 3, begin, count)
        if k < len(GROUPS) - 1:
            turn_rows(begin, count)
        return collect(begin, count)

    forward = []
    agg_h = jnp.zeros((256, 512), F32)
    for k, (begin, count) in enumerate(GROUPS):
        new = [p for p in range(begin, begin + count) if p]
        got([s2[p] for p in new])
        got([s2_r[p] for p in new])
        part = pl.ds(begin, count)
        sent = [copy(xall.at[0, part], xall.at[i, part], s_xf, begin * 4 + i, at(y, z, c, x + i)) for i in (2, 1, 3)]
        sent += [copy(rx.at[0, part], rx.at[i, part], s_rx, begin * 4 + i, at(y, z, c, x + i)) for i in (2, 1, 3)]
        forward.append(go(sent))
        edge_rows(0, 1, begin, count)
        if begin == GROUPS[1][0]:
            got(weights)
            loaded(7, 8)
            other = at(y, z, c + 1, x)
            shared = [copy(wni.at[half, :], wni.at[half, :], s_sh, 0, other)]
            for i in range(4):
                shared.append(copy(wno.at[quarter(i), :], wno.at[quarter(i), :], s_sh, 1 + i, other))
            go(shared)
        if begin == GROUPS[3][0]:
            got(shared)
            loaded(9, 10, 11)
            mesh = mesh_ref[...]
            z_mesh = mm(mesh, wni[0:512, :])
            w_both = mm_tn(weo_ref[...], wni[512:1024, :]).astype(BF)
            w_turn = mm(order, wni[512:1024, :]).astype(BF)
            w_last = wno[...].astype(F32)
            w_flat = (w_last - jnp.mean(w_last, axis=1, keepdims=True)).astype(BF)
            gain = gain_ref[...]
            up = cot_ref[...].astype(F32) * gain
            up = up - jnp.mean(up, axis=1, keepdims=True)
        if k >= LAG:
            agg_h += whole_group(k - LAG)

    for k in range(len(GROUPS) - LAG, len(GROUPS)):
        agg_h += whole_group(k)

    agg_h = agg_h.astype(BF)
    halves = (slice(0, 128), slice(128, 256))
    z_node = [z_mesh[h] + mm(agg_h[h], w_both) for h in halves]
    sig = [sigmoid(v) for v in z_node]
    h_node = [(v * s).astype(BF) for v, s in zip(z_node, sig)]
    centred = [mm(v, w_flat) for v in h_node]
    inv_std = [lax.rsqrt(jnp.mean(v * v, axis=1, keepdims=True) + 1e-05) for v in centred]
    normed = [v * s for v, s in zip(centred, inv_std)]
    d_y = [
        ((up[h] - v * jnp.mean(up[h] * v, axis=1, keepdims=True)) * s).astype(BF)
        for h, v, s in zip(halves, normed, inv_std)
    ]
    dz_node = [
        (mm_nt(d, wno[...]) * (s * (1.0 + v * (1.0 - s)))).astype(BF) for d, s, v in zip(d_y, sig, z_node)
    ]
    dh = jnp.concatenate([mm_nt(d, w_both).astype(BF) for d in dz_node], axis=0)
    d_agg = jnp.concatenate([mm_nt(d, w_turn).astype(BF) for d in dz_node], axis=0)

    turn_rows(*GROUPS[-1])
    d_edge = (mm(ct[...], dh) * sgrad[...]).astype(BF)
    acc[0] = mm(xt[...], d_edge)
    acc[1] = mm_tn(d_agg, agg_h)
    keep = pl.ds(pl.multiple_of(c * 64, 64), 64)
    give = pl.ds(pl.multiple_of((1 - c) * 64, 64), 64)
    core_src[...] = acc[:, give, :].astype(BF)
    to_core = go([copy(core_src, core_dst, s_core, 0, other)])
    for h, v in zip(halves, normed):
        nm[h, :] = (mesh[h].astype(F32) + v * gain).astype(BF)
    stored = pltpu.make_async_copy(nm, new_hbm, s_out)
    stored.start()

    got(to_core)
    acc[:, keep, :] += core_dst[...].astype(F32)
    for i in range(4):
        y_src[i] = acc[:, pl.ds(pl.multiple_of(c * 64 + i * 16, 16), 16), :].astype(BF)
    to_y = go([copy(y_src.at[(y + i) & 3], y_dst.at[i], s_y, i, at(y + i, z, c, x)) for i in (2, 1, 3)])
    got(to_y)
    rows = acc[:, pl.ds(pl.multiple_of(c * 64 + y * 16, 16), 16), :]
    for i in range(1, 4):
        rows += y_dst[i].astype(F32)
    for i in range(16):
        last_src[i, 0] = rows[0, i : i + 1]
        last_src[i, 1] = rows[1, i : i + 1]
    to_z = []
    for i in Z_LAST:
        to_z += go([copy(last_src.at[(z + i) & 15], last_dst.at[i], s_last, i, at(y, z + i, c, x))])
    total = last_src[z]
    for i in Z_AT[1:]:
        got([to_z[Z_LAST.index(i)]])
        total += last_dst[i]
    gin_ref[...] = total[0]
    gout_ref[...] = total[1]
    stored.wait()
    finish_all()


def body(
    grid_lat, edge_lat, send_local, dest_band, receiver_in_band, mesh_lat,
    w_edge_in, w_edge_out, w_node_in, w_node_out, norm_gain, cotangent,
):
    vmem = pl.BlockSpec(memory_space=pltpu.VMEM)
    dma = pltpu.SemaphoreType.DMA
    new_mesh, grad_in, grad_out = pl.pallas_call(
        kernel,
        out_shape=(
            jax.ShapeDtypeStruct((256, 512), BF),
            jax.ShapeDtypeStruct((1, 512), F32),
            jax.ShapeDtypeStruct((1, 512), F32),
        ),
        in_specs=[pl.BlockSpec(memory_space=pl.ANY)] * 12,
        out_specs=(pl.BlockSpec(memory_space=pl.ANY), vmem, vmem),
        scratch_shapes=[
            pltpu.VMEM((8, 32, 512), BF), pltpu.VMEM((8, 32, 512), BF),
            pltpu.VMEM((1, 128), F32), pltpu.VMEM((8, 1, 128), F32),
            pltpu.VMEM((16, 16, 512), BF), pltpu.VMEM((16, 1, 128), F32),
            pltpu.VMEM((4, 16, 16, 512), BF), pltpu.VMEM((4, 16, 1, 128), F32),
            pltpu.VMEM((128, 1024), BF), pltpu.VMEM((1024, 256), BF),
            pltpu.VMEM((1024, 512), BF), pltpu.VMEM((512, 512), BF),
            pltpu.VMEM((1024, 512), F32), pltpu.VMEM((1024, 512), BF), pltpu.VMEM((256, 512), BF),
            pltpu.VMEM((2, 64, 512), BF), pltpu.VMEM((2, 64, 512), BF),
            pltpu.VMEM((4, 2, 16, 512), BF), pltpu.VMEM((4, 2, 16, 512), BF),
            pltpu.VMEM((16, 2, 1, 512), F32), pltpu.VMEM((16, 2, 1, 512), F32), pltpu.VMEM((2, 128, 512), F32),
            pltpu.VMEM((1024, 512), BF), pltpu.VMEM((128, 512), BF),
            pltpu.VMEM((1, 128), I32), pltpu.VMEM((1, 128), I32), pltpu.VMEM((1, 128), I32),
            pltpu.VMEM((256, 512), BF), pltpu.VMEM((512, 512), BF), pltpu.VMEM((512, 512), BF),
            pltpu.VMEM((1, 512), F32), pltpu.VMEM((256, 512), BF),
            dma((12,)), dma, dma((2, 8)), dma((2, 8)), dma((2, 16)), dma((2, 16)), dma((2, 64)), dma((2, 64)),
            dma((2, 8)), dma((2, 5)), dma((2, 1)), dma((2, 4)), dma((2, 16)),
        ],
        compiler_params=pltpu.CompilerParams(
            collective_id=0, has_side_effects=True, vmem_limit_bytes=56 * 2**20
        ),
        name="encoder_step",
    )(
        grid_lat, edge_lat, send_local.reshape(1, 128), dest_band.reshape(1, 128), receiver_in_band.reshape(1, 128),
        mesh_lat, w_edge_in, w_edge_out, w_node_in, w_node_out, norm_gain.reshape(1, 512), cotangent,
    )
    return new_mesh, grad_in, grad_out


def solution(mesh):
    in_specs = (
        P("band", None),
        P(("band", "edge"), None),
        P(("band", "edge")),
        P(("band", "edge"), None),
        P(("band", "edge")),
        P("band", None),
        P(),
        P(),
        P(None, "edge"),
        P("edge", None),
        P(),
        P("band", None),
    )
    out_specs = (P("band", None), P(("band", "edge"), None), P(("band", "edge"), None))
    return jax.shard_map(body, mesh=mesh, in_specs=in_specs, out_specs=out_specs, check_vma=False)
```
